32 devices in a mesh: seq: 8 (over y, x, core), pipe: 4 (over z).
Axes of the slice: x: 2, y: 2, z: 4, core: 2. Of those that a mesh axis runs over, the one named last changes fastest.
Arguments:
- queries: bfloat16 [4, 1024, 12288], P('pipe', 'seq'), may hold values from -5.5 to 5.5
- keys: bfloat16 [4, 1024, 1024], P('pipe', 'seq'), may hold values from -5.5 to 5.5
- values: bfloat16 [4, 1024, 1024], P('pipe', 'seq'), may hold values from -6 to 6
- outputs: bfloat16 [4, 1024, 12288], P('pipe', 'seq'), may hold values from -3 to 3
- incoming: bfloat16 [4, 1024, 12288], P('pipe', 'seq'), may hold values from -6 to 6
- block_mask: int32 [4, 8, 8], P('pipe'), may hold values from 0 to 1, as said below
Outputs:
- grad_queries: bfloat16 [4, 1024, 12288], P('pipe', 'seq')
- grad_keys: bfloat16 [4, 1024, 1024], P('pipe', 'seq')
- grad_values: bfloat16 [4, 1024, 1024], P('pipe', 'seq')
The draws below stay inside these ranges and needn't reach their ends.
Inputs may be any that keep to these rules, and one draw needn't show every extreme that they name: block_mask[p, i, j] is 1 where query block i and key block j lie in the same passage, or where block i lies in the question, which takes the last 1 to max(1, 2) blocks of section p's sequence; else 0. Passages are runs of whole blocks before the question and differ from section to section.
All inputs are finite; a program needn't handle non-finite values.
Results may differ from the reference program's by a relative error of at most 0.0051.
Values may be sent and summed in bfloat16 or wider, within the bound.
A program may use at most 128 MiB of HBM per device.

```python
import jax
import jax.numpy as jnp
from jax import lax

H = 96
KVH = 8
DH = 128
SEQ = 1024
PIPE = 4


def draw_queries(key, part):
    key = jax.random.fold_in(key, 11)
    drawn = jnp.clip(jax.random.normal(key, (PIPE, SEQ, H, DH), jnp.float32), -4.5, 4.5)
    return drawn.reshape(PIPE, SEQ, H * DH).astype(jnp.bfloat16)


def draw_keys(key, part):
    key = jax.random.fold_in(key, 13)
    drawn = jnp.clip(jax.random.normal(key, (PIPE, SEQ, KVH, DH), jnp.float32), -4.5, 4.5)
    return drawn.reshape(PIPE, SEQ, KVH * DH).astype(jnp.bfloat16)


def draw_block_mask(key, part):
    key = jax.random.fold_in(key, 5)
    key_length, key_starts = jax.random.split(key)
    block_count = SEQ // 128
    question = jax.random.randint(key_length, (PIPE, 1), 1, max(1, block_count // 4) + 1)
    block_index = jnp.arange(block_count)
    starts = (jax.random.randint(key_starts, (PIPE, block_count), 0, 4) == 0) | (block_index[None, :] == 0)
    segment = jnp.cumsum(starts.astype(jnp.int32), axis=1)
    passage = block_index[None, :] < block_count - question
    same = (segment[:, :, None] == segment[:, None, :]) & passage[:, :, None] & passage[:, None, :]
    asking = jnp.broadcast_to(jnp.logical_not(passage)[:, :, None], (PIPE, block_count, block_count))
    return (same | asking).astype(jnp.int32)


def levels(key, shape, shards, smallest, top_value):
    def one(position, shards_of):
        heights = jax.random.uniform(jax.random.fold_in(jax.random.fold_in(key, 6), position), (shards_of,), jnp.float32, smallest / len(shards), top_value / len(shards))
        return jnp.repeat(jnp.exp(heights), shape[position] // shards_of).reshape((-1,) + (1,) * (len(shape) - position - 1))

    factor_of = one(*shards[0])
    for cut in shards[1:]:
        factor_of = factor_of * one(*cut)
    return factor_of


def noise(own_key, shape, deviation, reach, cuts=(), dtype=jnp.bfloat16):
    values = jax.random.normal(own_key, shape, jnp.float32) * deviation
    if len(cuts) > 0:
        values = levels(own_key, shape, cuts, -0.22, 0.18) * values
    return jnp.clip(values, min=-reach, max=reach).astype(dtype)


def setup_inputs(seed: int = 0) -> dict:
    streams_of = jax.random.split(jax.random.key(seed), 7)
    queries = draw_queries(jax.random.fold_in(streams_of[6], 71), 0)
    keys = draw_keys(jax.random.fold_in(streams_of[6], 71), 0)
    values = noise(streams_of[2], (PIPE, SEQ, KVH * DH), 1.0, 6.0, ((0, 4), (1, 8)))
    outputs = noise(streams_of[3], (PIPE, SEQ, H * DH), 0.5, 3.0, ((0, 4), (1, 8)))
    incoming = noise(streams_of[4], (PIPE, SEQ, H * DH), 1.0, 6.0, ((0, 4), (1, 8)))
    block_mask = draw_block_mask(jax.random.fold_in(streams_of[6], 71), 0)
    return dict(queries=queries, keys=keys, values=values, outputs=outputs, incoming=incoming, block_mask=block_mask)


NEG_FILL = -1e30


def head_grads(operands, allowed):
    q_head, k_head, v_head, o_head, g_head = operands
    scaling = DH ** -0.5
    q_full = q_head.astype(jnp.float32)
    k_full = k_head.astype(jnp.float32)
    v_full = v_head.astype(jnp.float32)
    o_full = o_head.astype(jnp.float32)
    g_full = g_head.astype(jnp.float32)
    logits = jnp.einsum("qgd,sd->gqs", q_full, k_full) * scaling
    masked = jnp.where(allowed[None], logits, NEG_FILL)
    row_max = jnp.max(masked, axis=-1)
    row_total = jnp.sum(jnp.where(allowed[None], jnp.exp(masked - row_max[..., None]), 0.0), axis=-1)
    log_total = row_max + jnp.log(row_total)
    weights = jnp.where(allowed[None], jnp.exp(logits - log_total[..., None]), 0.0)
    row_terms = jnp.sum(o_full * g_full, axis=-1).T
    dweights = jnp.einsum("qgd,sd->gqs", g_full, v_full)
    dlogits = lax.optimization_barrier((weights * (dweights - row_terms[..., None])).astype(jnp.bfloat16)).astype(jnp.float32)
    weights_low = lax.optimization_barrier(weights.astype(jnp.bfloat16)).astype(jnp.float32)
    grad_values = jnp.einsum("gqs,qgd->sd", weights_low, g_full)
    grad_keys = jnp.einsum("gqs,qgd->sd", dlogits, q_full) * scaling
    grad_queries = jnp.einsum("gqs,sd->qgd", dlogits, k_full) * scaling
    return grad_queries.astype(jnp.bfloat16), grad_keys.astype(jnp.bfloat16), grad_values.astype(jnp.bfloat16)


def section_grads(operands):
    queries, keys, values, outputs, cotangent, table = operands
    length = queries.shape[0]
    per_group = H // KVH
    positions = jnp.arange(length)
    block_ids = positions // 128
    allowed = (table[block_ids][:, block_ids] == 1) & (positions[None, :] <= positions[:, None])

    def split_heads(array):
        return jnp.moveaxis(array.reshape(length, KVH, per_group, DH), 1, 0)

    def split_kv(array):
        return jnp.moveaxis(array.reshape(length, KVH, DH), 1, 0)

    def one_head(operands_head):
        return head_grads(operands_head, allowed)

    grad_q, grad_k, grad_v = lax.map(one_head, (split_heads(queries), split_kv(keys), split_kv(values), split_heads(outputs), split_heads(cotangent)))
    grad_q = jnp.moveaxis(grad_q, 0, 1).reshape(length, H * DH)
    grad_k = jnp.moveaxis(grad_k, 0, 1).reshape(length, KVH * DH)
    grad_v = jnp.moveaxis(grad_v, 0, 1).reshape(length, KVH * DH)
    return grad_q, grad_k, grad_v


def reference(queries, keys, values, outputs, incoming, block_mask):
    cotangent = jnp.roll(incoming, -1, axis=0)
    grad_queries, grad_keys, grad_values = lax.map(section_grads, (queries, keys, values, outputs, cotangent, block_mask))
    return grad_queries, grad_keys, grad_values
```

```python
import functools
import math

import jax
import jax.numpy as jnp
from jax import lax
from jax.experimental import pallas as pl
from jax.experimental.pallas import tpu as pltpu
from jax.sharding import PartitionSpec as P

H = 96
KVH = 8
DH = 128
GROUP = H // KVH
WIDE = GROUP * DH
TILE_HEADS = 4
KEY_CHUNK = 256
AHEAD = 3
NEG_FILL = -1e30
MESH = pl.DeviceIdType.MESH
NT = (((1,), (1,)), ((), ()))
NN = (((1,), (0,)), ((), ()))


def dot(a, b, dims):
    return lax.dot_general(a, b, dims, preferred_element_type=jnp.float32)


def kernel(n, pipe, rows, q_hbm, k_hbm, v_hbm, o_hbm, g_hbm, mask_ref, dq_hbm, dk_ref, dv_ref,
           q_buf, o_buf, g_buf, dq_buf, k_buf, v_buf, kt_buf, bias, s_buf, acc_k, acc_v,
           stage, part, own, load_sem, self_sem, dq_sem, g_send, g_recv, kv_send, kv_recv,
           part_send, part_recv):
    me = lax.axis_index("seq")
    section = lax.axis_index("pipe")
    before = lax.rem(section + pipe - 1, pipe)
    after = lax.rem(section + 1, pipe)
    length = n * rows
    scaling = DH ** -0.5
    to_log2 = scaling * math.log2(math.e)

    def cols(c, width):
        return pl.ds(pl.multiple_of(c * width, width), width)

    def block(j):
        return pl.ds(pl.multiple_of(j * rows, rows), rows)

    def g_copy(c):
        return pltpu.make_async_remote_copy(
            src_ref=g_hbm.at[0, :, cols(c, WIDE)], dst_ref=g_buf.at[:, cols(c, WIDE)],
            send_sem=g_send.at[c], recv_sem=g_recv.at[c],
            device_id={"pipe": before}, device_id_type=MESH)

    def kv_copies(c, slot, peer):
        return [
            pltpu.make_async_remote_copy(
                src_ref=hbm.at[0, :, cols(c, DH)], dst_ref=buf.at[c, block(slot), :],
                send_sem=kv_send.at[w, c, peer], recv_sem=kv_recv.at[w, c, slot],
                device_id={"seq": peer}, device_id_type=MESH)
            for w, (hbm, buf) in enumerate(((k_hbm, k_buf), (v_hbm, v_buf)))
        ]

    def part_copy(c, slot, peer):
        return pltpu.make_async_remote_copy(
            src_ref=stage.at[c, block(peer), :], dst_ref=part.at[c, block(slot), :],
            send_sem=part_send.at[c, peer], recv_sem=part_recv.at[c, slot],
            device_id={"seq": peer}, device_id_type=MESH)

    def dq_copy(c):
        return pltpu.make_async_copy(
            dq_buf.at[:, cols(c, WIDE)], dq_hbm.at[0, :, cols(c, WIDE)], dq_sem.at[c])

    def self_copies(c):
        return [
            pltpu.make_async_copy(hbm.at[0, :, cols(c, DH)], buf.at[c, block(me), :], self_sem.at[w, c])
            for w, (hbm, buf) in enumerate(((k_hbm, k_buf), (v_hbm, v_buf)))
        ]

    barrier = pltpu.get_barrier_semaphore()

    def greet(d, carried):
        pl.semaphore_signal(barrier, inc=1, device_id={"seq": lax.rem(me + d, n)}, device_id_type=MESH)
        return carried

    lax.fori_loop(1, n, greet, 0)
    for neighbour in (before, after):
        pl.semaphore_signal(barrier, inc=1, device_id={"pipe": neighbour}, device_id_type=MESH)
    pl.semaphore_wait(barrier, n + 1)

    def send_group(c):
        g_copy(c).start()

        def to_peer(peer, carried):
            for copy in kv_copies(c, me, peer):
                copy.start()
            return carried

        lax.fori_loop(me + 1, n, to_peer, 0)

    q_load = pltpu.make_async_copy(q_hbm.at[0], q_buf, load_sem.at[0])
    o_load = pltpu.make_async_copy(o_hbm.at[0], o_buf, load_sem.at[1])

    def first_sends(c, carried):
        send_group(c)
        return carried

    lax.fori_loop(0, min(AHEAD, KVH), first_sends, 0)
    q_load.start()
    o_load.start()

    def own_block(c, carried):
        for copy in self_copies(c):
            copy.start()
        return carried

    lax.fori_loop(0, KVH, own_block, 0)

    def fill_bias(j, carried):
        k_pos = j * rows + lax.broadcasted_iota(jnp.int32, (rows, rows), 0)
        q_pos = me * rows + lax.broadcasted_iota(jnp.int32, (rows, rows), 1)
        closed = NEG_FILL * (1 - mask_ref[0, me, j]).astype(jnp.float32)
        bias[block(j), :] = jnp.where(k_pos <= q_pos, closed, NEG_FILL)
        return carried

    lax.fori_loop(0, n, fill_bias, 0)

    def clear(j, carried):
        k_buf[:, block(j), :] = jnp.zeros((KVH, rows, DH), jnp.bfloat16)
        v_buf[:, block(j), :] = jnp.zeros((KVH, rows, DH), jnp.bfloat16)
        return carried

    lax.fori_loop(me + 1, n, clear, 0)
    q_load.wait()
    o_load.wait()

    width = TILE_HEADS * rows
    chunks = length // KEY_CHUNK

    def group(c, carried):
        for copy in self_copies(c):
            copy.wait()

        def from_peer(slot, carried):
            for copy in kv_copies(c, slot, slot):
                copy.wait_recv()
            return carried

        lax.fori_loop(0, me, from_peer, 0)
        g_copy(c).wait_recv()

        @pl.when(c + AHEAD < KVH)
        def _():
            send_group(c + AHEAD)

        kt_buf[...] = k_buf[c].T
        acc_k[...] = jnp.zeros_like(acc_k)
        acc_v[...] = jnp.zeros_like(acc_v)

        def tile(t, carried):
            first = c * GROUP + t * TILE_HEADS

            def stacked(buf):
                return jnp.concatenate(
                    [buf[:, cols(first + i, DH)] for i in range(TILE_HEADS)], axis=0)

            q = stacked(q_buf)
            top = None
            for k in range(chunks):
                at = slice(k * KEY_CHUNK, (k + 1) * KEY_CHUNK)
                b = bias[at, :]
                s = dot(k_buf[c, at, :], q, NT) + jnp.concatenate([b] * TILE_HEADS, axis=1)
                s_buf[at, :] = s
                high = jnp.max(s.reshape(KEY_CHUNK // 8, 8, width), axis=0)
                top = high if top is None else jnp.maximum(top, high)
            top = jnp.max(top, axis=0, keepdims=True)
            total = None
            for k in range(chunks):
                at = slice(k * KEY_CHUNK, (k + 1) * KEY_CHUNK)
                p = jnp.exp2((s_buf[at, :] - top) * to_log2)
                s_buf[at, :] = p
                piece = jnp.sum(p.reshape(KEY_CHUNK // 8, 8, width), axis=0)
                total = piece if total is None else total + piece
            inverse = 1.0 / jnp.sum(total, axis=0, keepdims=True)
            g = stacked(g_buf)
            product = stacked(o_buf).astype(jnp.float32) * g.astype(jnp.float32)
            upper = product.astype(jnp.bfloat16)
            lower = (product - upper.astype(jnp.float32)).astype(jnp.bfloat16)
            ones = jnp.ones((8, DH), jnp.bfloat16)
            row_terms = (dot(ones, upper, NT) + dot(ones, lower, NT))[0:1]
            dqt = None
            for k in range(chunks):
                at = slice(k * KEY_CHUNK, (k + 1) * KEY_CHUNK)
                weights = s_buf[at, :] * inverse
                dw = dot(v_buf[c, at, :], g, NT)
                dl = (weights * (dw - row_terms)).astype(jnp.bfloat16)
                acc_v[at, :] += dot(weights.astype(jnp.bfloat16), g, NN)
                acc_k[at, :] += dot(dl, q, NN)
                piece = dot(kt_buf[:, at], dl, NN)
                dqt = piece if dqt is None else dqt + piece
            for i in range(TILE_HEADS):
                one = dqt[:, i * rows:(i + 1) * rows].T * scaling
                dq_buf[:, cols(first + i, DH)] = one.astype(jnp.bfloat16)
            return carried

        lax.fori_loop(0, GROUP // TILE_HEADS, tile, 0)
        dq_copy(c).start()
        stage[c, :, 0:DH] = (acc_k[...] * scaling).astype(jnp.bfloat16)
        stage[c, :, DH:2 * DH] = acc_v[...].astype(jnp.bfloat16)
        own[c, :, 0:DH] = acc_k[block(me), :] * scaling
        own[c, :, DH:2 * DH] = acc_v[block(me), :]

        def to_owner(peer, carried):
            part_copy(c, me, peer).start()
            return carried

        lax.fori_loop(0, me, to_owner, 0)
        return carried

    lax.fori_loop(0, KVH, group, 0)

    def finish(c, carried):
        def take(slot, total):
            part_copy(c, slot, slot).wait_recv()
            return total + part[c, block(slot), :].astype(jnp.float32)

        total = lax.fori_loop(me + 1, n, take, own[c]).astype(jnp.bfloat16)
        dk_ref[0, :, cols(c, DH)] = total[:, 0:DH]
        dv_ref[0, :, cols(c, DH)] = total[:, DH:2 * DH]
        return carried

    lax.fori_loop(0, KVH, finish, 0)

    def settle(c, carried):
        g_copy(c).wait_send()
        dq_copy(c).wait()

        def sent_kv(peer, carried):
            for copy in kv_copies(c, me, peer):
                copy.wait_send()
            return carried

        lax.fori_loop(me + 1, n, sent_kv, 0)

        def sent_part(peer, carried):
            part_copy(c, me, peer).wait_send()
            return carried

        lax.fori_loop(0, me, sent_part, 0)
        return carried

    lax.fori_loop(0, KVH, settle, 0)


def on_device(queries, keys, values, outputs, incoming, block_mask):
    n = lax.axis_size("seq")
    pipe = lax.axis_size("pipe")
    rows = queries.shape[1]
    length = n * rows
    anywhere = pl.BlockSpec(memory_space=pl.ANY)
    vmem = pl.BlockSpec(memory_space=pltpu.VMEM)
    low = jnp.bfloat16
    full = jnp.float32
    return pl.pallas_call(
        functools.partial(kernel, n, pipe, rows),
        out_shape=(
            jax.ShapeDtypeStruct(queries.shape, low),
            jax.ShapeDtypeStruct(keys.shape, low),
            jax.ShapeDtypeStruct(values.shape, low),
        ),
        in_specs=[anywhere] * 5 + [pl.BlockSpec(memory_space=pltpu.SMEM)],
        out_specs=(anywhere, vmem, vmem),
        scratch_shapes=[
            pltpu.VMEM((rows, H * DH), low),
            pltpu.VMEM((rows, H * DH), low),
            pltpu.VMEM((rows, H * DH), low),
            pltpu.VMEM((rows, H * DH), low),
            pltpu.VMEM((KVH, length, DH), low),
            pltpu.VMEM((KVH, length, DH), low),
            pltpu.VMEM((DH, length), low),
            pltpu.VMEM((length, rows), full),
            pltpu.VMEM((length, TILE_HEADS * rows), full),
            pltpu.VMEM((length, DH), full),
            pltpu.VMEM((length, DH), full),
            pltpu.VMEM((KVH, length, 2 * DH), low),
            pltpu.VMEM((KVH, length, 2 * DH), low),
            pltpu.VMEM((KVH, rows, 2 * DH), full),
            pltpu.SemaphoreType.DMA((2,)),
            pltpu.SemaphoreType.DMA((2, KVH)),
            pltpu.SemaphoreType.DMA((KVH,)),
            pltpu.SemaphoreType.DMA((KVH,)),
            pltpu.SemaphoreType.DMA((KVH,)),
            pltpu.SemaphoreType.DMA((2, KVH, n)),
            pltpu.SemaphoreType.DMA((2, KVH, n)),
            pltpu.SemaphoreType.DMA((KVH, n)),
            pltpu.SemaphoreType.DMA((KVH, n)),
        ],
        compiler_params=pltpu.CompilerParams(
            collective_id=0, has_side_effects=True, vmem_limit_bytes=58 * 1024 * 1024),
        cost_estimate=pl.CostEstimate(
            flops=10 * rows * length * H * DH,
            bytes_accessed=5 * rows * H * DH * 2,
            transcendentals=rows * length * H),
    )(queries, keys, values, outputs, incoming, block_mask)


def solution(mesh):
    placed = (
        P("pipe", "seq", None),
        P("pipe", "seq", None),
        P("pipe", "seq", None),
        P("pipe", "seq", None),
        P("pipe", "seq", None),
        P("pipe", None, None),
    )
    return jax.shard_map(
        on_device,
        mesh=mesh,
        in_specs=placed,
        out_specs=(P("pipe", "seq", None), P("pipe", "seq", None), P("pipe", "seq", None)),
        check_vma=False,
    )
```

```python
import functools
import math

import jax
import jax.numpy as jnp
from jax import lax
from jax.experimental import pallas as pl
from jax.experimental.pallas import tpu as pltpu
from jax.sharding import PartitionSpec as P

H = 96
KVH = 8
DH = 128
GROUP = H // KVH
WIDE = GROUP * DH
TILE_HEADS = 4
KEY_CHUNK = 256
TILES = GROUP // TILE_HEADS
CHUNK = TILE_HEADS * DH
PARTS = KVH * TILES
KV_AHEAD = 2
G_AHEAD = 6
NEG_FILL = -1e30
MESH = pl.DeviceIdType.MESH
NT = (((1,), (1,)), ((), ()))
NN = (((1,), (0,)), ((), ()))


def dot(a, b, dims):
    return lax.dot_general(a, b, dims, preferred_element_type=jnp.float32)


def kernel(n, pipe, rows, q_hbm, k_hbm, v_hbm, o_hbm, g_hbm, mask_hbm, dq_ref, dk_ref, dv_ref,
           mask_ref, q_buf, o_buf, g_buf, k_buf, v_buf, kt_buf, bias, s_buf, acc_k, acc_v,
           stage, part, own, load_sem, self_sem, g_send, g_recv, kv_send, kv_recv,
           part_send, part_recv):
    me = lax.axis_index("seq")
    section = lax.axis_index("pipe")
    before = lax.rem(section + pipe - 1, pipe)
    after = lax.rem(section + 1, pipe)
    length = n * rows
    scaling = DH ** -0.5
    to_log2 = scaling * math.log2(math.e)

    def cols(c, width):
        return pl.ds(pl.multiple_of(c * width, width), width)

    def block(j):
        return pl.ds(pl.multiple_of(j * rows, rows), rows)

    def g_copy(c):
        return pltpu.make_async_remote_copy(
            src_ref=g_hbm.at[0, :, cols(c, CHUNK)], dst_ref=g_buf.at[:, cols(c, CHUNK)],
            send_sem=g_send.at[c], recv_sem=g_recv.at[c],
            device_id={"pipe": before}, device_id_type=MESH)

    def kv_copies(c, slot, peer):
        return [
            pltpu.make_async_remote_copy(
                src_ref=hbm.at[0, :, cols(c, DH)], dst_ref=buf.at[c, block(slot), :],
                send_sem=kv_send.at[w, c, peer], recv_sem=kv_recv.at[w, c, slot],
                device_id={"seq": peer}, device_id_type=MESH)
            for w, (hbm, buf) in enumerate(((k_hbm, k_buf), (v_hbm, v_buf)))
        ]

    def part_copy(c, slot, peer):
        return pltpu.make_async_remote_copy(
            src_ref=stage.at[c, block(peer), :], dst_ref=part.at[c, block(slot), :],
            send_sem=part_send.at[c, peer], recv_sem=part_recv.at[c, slot],
            device_id={"seq": peer}, device_id_type=MESH)

    def self_copies(c):
        return [
            pltpu.make_async_copy(hbm.at[0, :, cols(c, DH)], buf.at[c, block(me), :], self_sem.at[w, c])
            for w, (hbm, buf) in enumerate(((k_hbm, k_buf), (v_hbm, v_buf)))
        ]

    barrier = pltpu.get_barrier_semaphore()

    def greet(d, carried):
        pl.semaphore_signal(barrier, inc=1, device_id={"seq": lax.rem(me + d, n)}, device_id_type=MESH)
        return carried

    lax.fori_loop(1, n, greet, 0)
    for neighbour in (before, after):
        pl.semaphore_signal(barrier, inc=1, device_id={"pipe": neighbour}, device_id_type=MESH)
    pl.semaphore_wait(barrier, n + 1)

    def send_keys(c):
        def to_peer(peer, carried):
            for copy in kv_copies(c, me, peer):
                copy.start()
            return carried

        lax.fori_loop(me + 1, n, to_peer, 0)

    def send_grads(c, carried):
        g_copy(c).start()
        return carried

    mask_load = pltpu.make_async_copy(mask_hbm, mask_ref, load_sem.at[2])
    mask_load.start()
    q_load = pltpu.make_async_copy(q_hbm.at[0], q_buf, load_sem.at[0])
    o_load = pltpu.make_async_copy(o_hbm.at[0], o_buf, load_sem.at[1])

    lax.fori_loop(0, G_AHEAD, send_grads, 0)
    for c in range(KV_AHEAD):
        send_keys(c)
    q_load.start()
    o_load.start()

    def own_block(c, carried):
        for copy in self_copies(c):
            copy.start()
        return carried

    lax.fori_loop(0, KVH, own_block, 0)

    def fill_bias(j, carried):
        k_pos = j * rows + lax.broadcasted_iota(jnp.int32, (rows, rows), 0)
        q_pos = me * rows + lax.broadcasted_iota(jnp.int32, (rows, rows), 1)
        closed = NEG_FILL * (1 - mask_ref[0, me, j]).astype(jnp.float32)
        bias[block(j), :] = jnp.where(k_pos <= q_pos, closed, NEG_FILL)
        return carried

    mask_load.wait()
    lax.fori_loop(0, n, fill_bias, 0)

    def clear(j, carried):
        k_buf[:, block(j), :] = jnp.zeros((KVH, rows, DH), jnp.bfloat16)
        v_buf[:, block(j), :] = jnp.zeros((KVH, rows, DH), jnp.bfloat16)
        return carried

    lax.fori_loop(me + 1, n, clear, 0)
    q_load.wait()
    o_load.wait()

    width = TILE_HEADS * rows
    chunks = length // KEY_CHUNK

    def finish(c):
        def take(slot, total):
            part_copy(c, slot, slot).wait_recv()
            return total + part[c, block(slot), :].astype(jnp.float32)

        total = lax.fori_loop(me + 1, n, take, own[c]).astype(jnp.bfloat16)
        dk_ref[0, :, cols(c, DH)] = total[:, 0:DH]
        dv_ref[0, :, cols(c, DH)] = total[:, DH:2 * DH]

    def group(c, carried):
        for copy in self_copies(c):
            copy.wait()

        def from_peer(slot, carried):
            for copy in kv_copies(c, slot, slot):
                copy.wait_recv()
            return carried

        lax.fori_loop(0, me, from_peer, 0)

        @pl.when(c + KV_AHEAD < KVH)
        def _():
            send_keys(c + KV_AHEAD)

        @pl.when(c >= 2)
        def _():
            finish(c - 2)

        kt_buf[...] = k_buf[c].T
        acc_k[...] = jnp.zeros_like(acc_k)
        acc_v[...] = jnp.zeros_like(acc_v)

        def tile(t, carried):
            first = c * GROUP + t * TILE_HEADS

            def stacked(buf):
                return jnp.concatenate(
                    [buf[:, cols(first + i, DH)] for i in range(TILE_HEADS)], axis=0)

            q = stacked(q_buf)
            top = None
            for k in range(chunks):
                at = slice(k * KEY_CHUNK, (k + 1) * KEY_CHUNK)
                b = bias[at, :]
                s = dot(k_buf[c, at, :], q, NT) + jnp.concatenate([b] * TILE_HEADS, axis=1)
                s_buf[at, :] = s
                high = jnp.max(s.reshape(KEY_CHUNK // 8, 8, width), axis=0)
                top = high if top is None else jnp.maximum(top, high)
            top = jnp.max(top, axis=0, keepdims=True)
            total = None
            for k in range(chunks):
                at = slice(k * KEY_CHUNK, (k + 1) * KEY_CHUNK)
                p = jnp.exp2((s_buf[at, :] - top) * to_log2)
                s_buf[at, :] = p
                piece = jnp.sum(p.reshape(KEY_CHUNK // 8, 8, width), axis=0)
                total = piece if total is None else total + piece
            inverse = 1.0 / jnp.sum(total, axis=0, keepdims=True)
            now = c * TILES + t
            g_copy(now).wait_recv()

            @pl.when(now + G_AHEAD < PARTS)
            def _():
                g_copy(now + G_AHEAD).start()

            g = stacked(g_buf)
            product = stacked(o_buf).astype(jnp.float32) * g.astype(jnp.float32)
            upper = product.astype(jnp.bfloat16)
            lower = (product - upper.astype(jnp.float32)).astype(jnp.bfloat16)
            ones = jnp.ones((8, DH), jnp.bfloat16)
            row_terms = (dot(ones, upper, NT) + dot(ones, lower, NT))[0:1]
            dqt = None
            for k in range(chunks):
                at = slice(k * KEY_CHUNK, (k + 1) * KEY_CHUNK)
                weights = s_buf[at, :] * inverse
                dw = dot(v_buf[c, at, :], g, NT)
                dl = (weights * (dw - row_terms)).astype(jnp.bfloat16)
                acc_v[at, :] += dot(weights.astype(jnp.bfloat16), g, NN)
                acc_k[at, :] += dot(dl, q, NN)
                piece = dot(kt_buf[:, at], dl, NN)
                dqt = piece if dqt is None else dqt + piece
            for i in range(TILE_HEADS):
                one = dqt[:, i * rows:(i + 1) * rows].T * scaling
                dq_ref[0, :, cols(first + i, DH)] = one.astype(jnp.bfloat16)
            return carried

        lax.fori_loop(0, TILES, tile, 0)
        stage[c, :, 0:DH] = (acc_k[...] * scaling).astype(jnp.bfloat16)
        stage[c, :, DH:2 * DH] = acc_v[...].astype(jnp.bfloat16)
        own[c, :, 0:DH] = acc_k[block(me), :] * scaling
        own[c, :, DH:2 * DH] = acc_v[block(me), :]

        def to_owner(peer, carried):
            part_copy(c, me, peer).start()
            return carried

        lax.fori_loop(0, me, to_owner, 0)
        return carried

    lax.fori_loop(0, KVH, group, 0)

    finish(KVH - 2)
    finish(KVH - 1)

    def settle(c, carried):
        def sent_kv(peer, carried):
            for copy in kv_copies(c, me, peer):
                copy.wait_send()
            return carried

        lax.fori_loop(me + 1, n, sent_kv, 0)

        def sent_part(peer, carried):
            part_copy(c, me, peer).wait_send()
            return carried

        lax.fori_loop(0, me, sent_part, 0)
        return carried

    lax.fori_loop(0, KVH, settle, 0)

    def sent_grads(c, carried):
        g_copy(c).wait_send()
        return carried

    lax.fori_loop(0, PARTS, sent_grads, 0)


def write_out(*refs):
    sources, targets, sems = refs[0:3], refs[3:6], refs[6]
    copies = [
        pltpu.make_async_copy(source, target, sems.at[w])
        for w, (source, target) in enumerate(zip(sources, targets))
    ]
    for copy in copies:
        copy.start()
    for copy in copies:
        copy.wait()


def on_device(queries, keys, values, outputs, incoming, block_mask):
    n = lax.axis_size("seq")
    pipe = lax.axis_size("pipe")
    rows = queries.shape[1]
    length = n * rows
    vmem = pl.BlockSpec(memory_space=pltpu.VMEM)
    low = jnp.bfloat16
    full = jnp.float32
    grads = pl.pallas_call(
        functools.partial(kernel, n, pipe, rows),
        out_shape=(
            pltpu.VMEM(queries.shape, low),
            pltpu.VMEM(keys.shape, low),
            pltpu.VMEM(values.shape, low),
        ),
        in_specs=[pl.BlockSpec(memory_space=pltpu.HBM)] * 6,
        out_specs=(vmem, vmem, vmem),
        scratch_shapes=[
            pltpu.SMEM(block_mask.shape, jnp.int32),
            pltpu.VMEM((rows, H * DH), low),
            pltpu.VMEM((rows, H * DH), low),
            pltpu.VMEM((rows, H * DH), low),
            pltpu.VMEM((KVH, length, DH), low),
            pltpu.VMEM((KVH, length, DH), low),
            pltpu.VMEM((DH, length), low),
            pltpu.VMEM((length, rows), full),
            pltpu.VMEM((length, TILE_HEADS * rows), full),
            pltpu.VMEM((length, DH), full),
            pltpu.VMEM((length, DH), full),
            pltpu.VMEM((KVH, length, 2 * DH), low),
            pltpu.VMEM((KVH, length, 2 * DH), low),
            pltpu.VMEM((KVH, rows, 2 * DH), full),
            pltpu.SemaphoreType.DMA((3,)),
            pltpu.SemaphoreType.DMA((2, KVH)),
            pltpu.SemaphoreType.DMA((PARTS,)),
            pltpu.SemaphoreType.DMA((PARTS,)),
            pltpu.SemaphoreType.DMA((2, KVH, n)),
            pltpu.SemaphoreType.DMA((2, KVH, n)),
            pltpu.SemaphoreType.DMA((KVH, n)),
            pltpu.SemaphoreType.DMA((KVH, n)),
        ],
        compiler_params=pltpu.CompilerParams(
            collective_id=0, has_side_effects=True, vmem_limit_bytes=52 * 1024 * 1024),
        cost_estimate=pl.CostEstimate(
            flops=10 * rows * length * H * DH,
            bytes_accessed=5 * rows * H * DH * 2,
            transcendentals=rows * length * H),
    )(queries, keys, values, outputs, incoming, block_mask)
    return pl.pallas_call(
        write_out,
        out_shape=[jax.ShapeDtypeStruct(grad.shape, low) for grad in grads],
        in_specs=[vmem] * 3,
        out_specs=[pl.BlockSpec(memory_space=pltpu.HBM)] * 3,
        scratch_shapes=[pltpu.SemaphoreType.DMA((3,))],
        compiler_params=pltpu.CompilerParams(vmem_limit_bytes=1024 * 1024),
    )(*grads)


def solution(mesh):
    placed = (
        P("pipe", "seq", None),
        P("pipe", "seq", None),
        P("pipe", "seq", None),
        P("pipe", "seq", None),
        P("pipe", "seq", None),
        P("pipe", None, None),
    )
    return jax.shard_map(
        on_device,
        mesh=mesh,
        in_specs=placed,
        out_specs=(P("pipe", "seq", None), P("pipe", "seq", None), P("pipe", "seq", None)),
        check_vma=False,
    )
```

```python
import functools
import math

import jax
import jax.numpy as jnp
from jax import lax
from jax.experimental import pallas as pl
from jax.experimental.pallas import tpu as pltpu
from jax.sharding import PartitionSpec as P

H = 96
KVH = 8
DH = 128
GROUP = H // KVH
WIDE = GROUP * DH
TILE_HEADS = 4
KEY_CHUNK = 256
TILES = GROUP // TILE_HEADS
CHUNK = TILE_HEADS * DH
PARTS = KVH * TILES
KV_AHEAD = 2
G_AHEAD = 6
NEG_FILL = -1e30
MESH = pl.DeviceIdType.MESH
NT = (((1,), (1,)), ((), ()))
NN = (((1,), (0,)), ((), ()))


def dot(a, b, dims):
    return lax.dot_general(a, b, dims, preferred_element_type=jnp.float32)


def kernel(n, pipe, rows, q_hbm, k_hbm, v_hbm, o_hbm, g_hbm, mask_hbm, dq_ref, dk_ref, dv_ref,
           mask_ref, q_buf, o_buf, g_buf, k_buf, v_buf, kt_buf, bias, s_buf, acc_k, acc_v,
           stage, part, own, load_sem, self_sem, g_send, g_recv, kv_send, kv_recv,
           part_send, part_recv):
    me = lax.axis_index("seq")
    section = lax.axis_index("pipe")
    before = lax.rem(section + pipe - 1, pipe)
    after = lax.rem(section + 1, pipe)
    length = n * rows
    scaling = DH ** -0.5
    to_log2 = scaling * math.log2(math.e)

    def cols(c, width):
        return pl.ds(pl.multiple_of(c * width, width), width)

    def block(j):
        return pl.ds(pl.multiple_of(j * rows, rows), rows)

    def g_copy(c):
        return pltpu.make_async_remote_copy(
            src_ref=g_hbm.at[0, :, cols(c, CHUNK)], dst_ref=g_buf.at[:, cols(c, CHUNK)],
            send_sem=g_send.at[c], recv_sem=g_recv.at[c],
            device_id={"pipe": before}, device_id_type=MESH)

    def kv_copies(c, slot, peer):
        return [
            pltpu.make_async_remote_copy(
                src_ref=hbm.at[0, :, cols(c, DH)], dst_ref=buf.at[c, block(slot), :],
                send_sem=kv_send.at[w, c, peer], recv_sem=kv_recv.at[w, c, slot],
                device_id={"seq": peer}, device_id_type=MESH)
            for w, (hbm, buf) in enumerate(((k_hbm, k_buf), (v_hbm, v_buf)))
        ]

    def part_copy(c, slot, peer):
        return pltpu.make_async_remote_copy(
            src_ref=stage.at[c, block(peer), :], dst_ref=part.at[c, block(slot), :],
            send_sem=part_send.at[c, peer], recv_sem=part_recv.at[c, slot],
            device_id={"seq": peer}, device_id_type=MESH)

    def self_copies(c):
        return [
            pltpu.make_async_copy(hbm.at[0, :, cols(c, DH)], buf.at[c, block(me), :], self_sem.at[w, c])
            for w, (hbm, buf) in enumerate(((k_hbm, k_buf), (v_hbm, v_buf)))
        ]

    barrier = pltpu.get_barrier_semaphore()

    def greet(d, carried):
        pl.semaphore_signal(barrier, inc=1, device_id={"seq": lax.rem(me + d, n)}, device_id_type=MESH)
        return carried

    lax.fori_loop(1, n, greet, 0)
    for neighbour in (before, after):
        pl.semaphore_signal(barrier, inc=1, device_id={"pipe": neighbour}, device_id_type=MESH)
    pl.semaphore_wait(barrier, n + 1)

    def send_keys(c):
        def to_peer(peer, carried):
            for copy in kv_copies(c, me, peer):
                copy.start()
            return carried

        lax.fori_loop(me + 1, n, to_peer, 0)

    def send_grads(c, carried):
        g_copy(c).start()
        return carried

    mask_load = pltpu.make_async_copy(mask_hbm, mask_ref, load_sem.at[2])
    mask_load.start()
    q_load = pltpu.make_async_copy(q_hbm.at[0], q_buf, load_sem.at[0])
    o_load = pltpu.make_async_copy(o_hbm.at[0], o_buf, load_sem.at[1])

    lax.fori_loop(0, G_AHEAD, send_grads, 0)
    for c in range(KV_AHEAD):
        send_keys(c)
    q_load.start()
    o_load.start()

    def own_block(c, carried):
        for copy in self_copies(c):
            copy.start()
        return carried

    lax.fori_loop(0, KVH, own_block, 0)

    def fill_bias(j, carried):
        k_pos = j * rows + lax.broadcasted_iota(jnp.int32, (rows, rows), 0)
        q_pos = me * rows + lax.broadcasted_iota(jnp.int32, (rows, rows), 1)
        closed = NEG_FILL * (1 - mask_ref[0, me, j]).astype(jnp.float32)
        bias[block(j), :] = jnp.where(k_pos <= q_pos, closed, NEG_FILL)
        return carried

    mask_load.wait()
    lax.fori_loop(0, n, fill_bias, 0)

    def clear(j, carried):
        k_buf[:, block(j), :] = jnp.zeros((KVH, rows, DH), jnp.bfloat16)
        v_buf[:, block(j), :] = jnp.zeros((KVH, rows, DH), jnp.bfloat16)
        return carried

    lax.fori_loop(me + 1, n, clear, 0)
    q_load.wait()
    o_load.wait()

    width = TILE_HEADS * rows
    chunks = length // KEY_CHUNK

    def finish(c):
        def take(slot, total):
            part_copy(c, slot, slot).wait_recv()
            return total + part[c, block(slot), :].astype(jnp.float32)

        total = lax.fori_loop(me + 1, n, take, own[c]).astype(jnp.bfloat16)
        dk_ref[0, :, cols(c, DH)] = total[:, 0:DH]
        dv_ref[0, :, cols(c, DH)] = total[:, DH:2 * DH]

    def group(c, carried):
        for copy in self_copies(c):
            copy.wait()

        def from_peer(slot, carried):
            for copy in kv_copies(c, slot, slot):
                copy.wait_recv()
            return carried

        lax.fori_loop(0, me, from_peer, 0)

        @pl.when(c + KV_AHEAD < KVH)
        def _():
            send_keys(c + KV_AHEAD)

        @pl.when(c >= 2)
        def _():
            finish(c - 2)

        kt_buf[...] = k_buf[c].T
        acc_k[...] = jnp.zeros_like(acc_k)
        acc_v[...] = jnp.zeros_like(acc_v)

        def to_owner(peer, carried):
            part_copy(c, me, peer).start()
            return carried

        def tile(t, carried, last=False):
            first = c * GROUP + t * TILE_HEADS

            def stacked(buf):
                return jnp.concatenate(
                    [buf[:, cols(first + i, DH)] for i in range(TILE_HEADS)], axis=0)

            q = stacked(q_buf)
            top = None
            for k in range(chunks):
                at = slice(k * KEY_CHUNK, (k + 1) * KEY_CHUNK)
                b = bias[at, :]
                s = dot(k_buf[c, at, :], q, NT) + jnp.concatenate([b] * TILE_HEADS, axis=1)
                s_buf[at, :] = s
                high = jnp.max(s.reshape(KEY_CHUNK // 8, 8, width), axis=0)
                top = high if top is None else jnp.maximum(top, high)
            top = jnp.max(top, axis=0, keepdims=True)
            total = None
            for k in range(chunks):
                at = slice(k * KEY_CHUNK, (k + 1) * KEY_CHUNK)
                p = jnp.exp2((s_buf[at, :] - top) * to_log2)
                s_buf[at, :] = p
                piece = jnp.sum(p.reshape(KEY_CHUNK // 8, 8, width), axis=0)
                total = piece if total is None else total + piece
            inverse = 1.0 / jnp.sum(total, axis=0, keepdims=True)
            now = c * TILES + t
            g_copy(now).wait_recv()

            @pl.when(now + G_AHEAD < PARTS)
            def _():
                g_copy(now + G_AHEAD).start()

            g = stacked(g_buf)
            product = stacked(o_buf).astype(jnp.float32) * g.astype(jnp.float32)
            upper = product.astype(jnp.bfloat16)
            lower = (product - upper.astype(jnp.float32)).astype(jnp.bfloat16)
            ones = jnp.ones((8, DH), jnp.bfloat16)
            row_terms = (dot(ones, upper, NT) + dot(ones, lower, NT))[0:1]
            dqt = None
            for k in range(chunks):
                at = slice(k * KEY_CHUNK, (k + 1) * KEY_CHUNK)
                weights = s_buf[at, :] * inverse
                dw = dot(v_buf[c, at, :], g, NT)
                dl = (weights * (dw - row_terms)).astype(jnp.bfloat16)
                acc_v[at, :] += dot(weights.astype(jnp.bfloat16), g, NN)
                acc_k[at, :] += dot(dl, q, NN)
                piece = dot(kt_buf[:, at], dl, NN)
                dqt = piece if dqt is None else dqt + piece
                if last:
                    stage[c, at, 0:DH] = (acc_k[at, :] * scaling).astype(jnp.bfloat16)
                    stage[c, at, DH:2 * DH] = acc_v[at, :].astype(jnp.bfloat16)
                    if k == chunks // 2 - 1:
                        lax.fori_loop(0, jnp.minimum(me, n // 2), to_owner, 0)
            if last:
                lax.fori_loop(n // 2, me, to_owner, 0)
            for i in range(TILE_HEADS):
                one = dqt[:, i * rows:(i + 1) * rows].T * scaling
                dq_ref[0, :, cols(first + i, DH)] = one.astype(jnp.bfloat16)
            return carried

        lax.fori_loop(0, TILES - 1, tile, 0)
        tile(TILES - 1, 0, True)
        own[c, :, 0:DH] = acc_k[block(me), :] * scaling
        own[c, :, DH:2 * DH] = acc_v[block(me), :]

        return carried

    lax.fori_loop(0, KVH, group, 0)

    finish(KVH - 2)
    finish(KVH - 1)

    def settle(c, carried):
        def sent_kv(peer, carried):
            for copy in kv_copies(c, me, peer):
                copy.wait_send()
            return carried

        lax.fori_loop(me + 1, n, sent_kv, 0)

        def sent_part(peer, carried):
            part_copy(c, me, peer).wait_send()
            return carried

        lax.fori_loop(0, me, sent_part, 0)
        return carried

    lax.fori_loop(0, KVH, settle, 0)

    def sent_grads(c, carried):
        g_copy(c).wait_send()
        return carried

    lax.fori_loop(0, PARTS, sent_grads, 0)


def write_out(*refs):
    sources, targets, sems = refs[0:3], refs[3:6], refs[6]
    copies = [
        pltpu.make_async_copy(source, target, sems.at[w])
        for w, (source, target) in enumerate(zip(sources, targets))
    ]
    for copy in copies:
        copy.start()
    for copy in copies:
        copy.wait()


def on_device(queries, keys, values, outputs, incoming, block_mask):
    n = lax.axis_size("seq")
    pipe = lax.axis_size("pipe")
    rows = queries.shape[1]
    length = n * rows
    vmem = pl.BlockSpec(memory_space=pltpu.VMEM)
    low = jnp.bfloat16
    full = jnp.float32
    grads = pl.pallas_call(
        functools.partial(kernel, n, pipe, rows),
        out_shape=(
            pltpu.VMEM(queries.shape, low),
            pltpu.VMEM(keys.shape, low),
            pltpu.VMEM(values.shape, low),
        ),
        in_specs=[pl.BlockSpec(memory_space=pltpu.HBM)] * 6,
        out_specs=(vmem, vmem, vmem),
        scratch_shapes=[
            pltpu.SMEM(block_mask.shape, jnp.int32),
            pltpu.VMEM((rows, H * DH), low),
            pltpu.VMEM((rows, H * DH), low),
            pltpu.VMEM((rows, H * DH), low),
            pltpu.VMEM((KVH, length, DH), low),
            pltpu.VMEM((KVH, length, DH), low),
            pltpu.VMEM((DH, length), low),
            pltpu.VMEM((length, rows), full),
            pltpu.VMEM((length, TILE_HEADS * rows), full),
            pltpu.VMEM((length, DH), full),
            pltpu.VMEM((length, DH), full),
            pltpu.VMEM((KVH, length, 2 * DH), low),
            pltpu.VMEM((KVH, length, 2 * DH), low),
            pltpu.VMEM((KVH, rows, 2 * DH), full),
            pltpu.SemaphoreType.DMA((3,)),
            pltpu.SemaphoreType.DMA((2, KVH)),
            pltpu.SemaphoreType.DMA((PARTS,)),
            pltpu.SemaphoreType.DMA((PARTS,)),
            pltpu.SemaphoreType.DMA((2, KVH, n)),
            pltpu.SemaphoreType.DMA((2, KVH, n)),
            pltpu.SemaphoreType.DMA((KVH, n)),
            pltpu.SemaphoreType.DMA((KVH, n)),
        ],
        compiler_params=pltpu.CompilerParams(
            collective_id=0, has_side_effects=True, vmem_limit_bytes=52 * 1024 * 1024),
        cost_estimate=pl.CostEstimate(
            flops=10 * rows * length * H * DH,
            bytes_accessed=5 * rows * H * DH * 2,
            transcendentals=rows * length * H),
    )(queries, keys, values, outputs, incoming, block_mask)
    return pl.pallas_call(
        write_out,
        out_shape=[jax.ShapeDtypeStruct(grad.shape, low) for grad in grads],
        in_specs=[vmem] * 3,
        out_specs=[pl.BlockSpec(memory_space=pltpu.HBM)] * 3,
        scratch_shapes=[pltpu.SemaphoreType.DMA((3,))],
        compiler_params=pltpu.CompilerParams(vmem_limit_bytes=1024 * 1024),
    )(*grads)


def solution(mesh):
    placed = (
        P("pipe", "seq", None),
        P("pipe", "seq", None),
        P("pipe", "seq", None),
        P("pipe", "seq", None),
        P("pipe", "seq", None),
        P("pipe", None, None),
    )
    return jax.shard_map(
        on_device,
        mesh=mesh,
        in_specs=placed,
        out_specs=(P("pipe", "seq", None), P("pipe", "seq", None), P("pipe", "seq", None)),
        check_vma=False,
    )
```
